512 devices in a mesh: tm: 32 (over x_lo, z), space: 16 (over x_hi, y, core).
Axes of the slice: x: 4 (x_hi: 2, x_lo: 2; x = x_hi * 2 + x_lo), y: 4, z: 16, core: 2. Of those that a mesh axis runs over, the one named last changes fastest.
Arguments:
- iterate: float32 [32, 512, 4096], P('tm', 'space'), may hold values from -6 to 6
- source: float32 [32, 512, 4096], P('tm', 'space'), may hold values from -6 to 6
- conduct: float32 [512, 4096], P('space'), may hold values from 0.2 to 5
Outputs:
- updated: float32 [32, 512, 4096], P('tm', 'space')
The draws below stay inside these ranges and needn't reach their ends.
All inputs are finite; a program needn't handle non-finite values.
Results may differ from the reference program's by a relative error of at most 0.0003.
Values sent between devices are 32-bit elements; how exact they have to be, the bound alone decides.
A program may use at most 64 MiB of HBM per device.

```python
import math
import jax
import jax.numpy as jnp
from jax import lax

NC = 4096
SWEEPS = 8
STEPS = 32
NR = 512


def level_of(own_key, shape, shards, low, largest):
    level, own = 1.0, jax.random.fold_in(own_key, 6)
    for position, shards_of in shards:
        steps = jnp.exp(jax.random.uniform(jax.random.fold_in(own, position), (shards_of,), jnp.float32, low / len(shards), largest / len(shards)))
        level = level * jnp.repeat(steps, shape[position] // shards_of).reshape([-1 if axis == position else 1 for axis in range(len(shape))])
    return level


def normal_values(stream_key, shape, width, reach, cuts=(), held_as=jnp.bfloat16):
    drawn = width * jax.random.normal(stream_key, shape, jnp.float32)
    if cuts:
        drawn = drawn * level_of(stream_key, shape, cuts, -0.22, 0.18)
    return jnp.clip(drawn, -reach, reach).astype(held_as)


def setup_inputs(seed: int = 0) -> dict:
    keys = jax.random.split(jax.random.key(seed), 4)
    return {
        "iterate": normal_values(keys[0], (STEPS, NR, NC), 1.0, 6.0, ((0, 32), (1, 16)), jnp.float32),
        "source": normal_values(keys[1], (STEPS, NR, NC), 1.0, 6.0, ((0, 32), (1, 16)), jnp.float32),
        "conduct": jnp.clip(jnp.exp(math.log(5.0) - 3.218876 * jax.random.uniform(keys[2], (NR, NC), jnp.float32) ** level_of(keys[2], (NR, NC), ((0, 16),), -0.2, 0.2)), 0.2, 5.0),
    }


ALPHA = 0.05
OMEGA = 0.8


def face_terms(conduct_rows):
    middle = conduct_rows[1:-1]
    up_face = 0.5 * (middle + conduct_rows[:-2])
    down_face = 0.5 * (middle + conduct_rows[2:])
    padded = jnp.pad(middle, ((0, 0), (1, 1)))
    left_face = 0.5 * (middle + padded[:, :-2])
    right_face = 0.5 * (middle + padded[:, 2:])
    return up_face, down_face, left_face, right_face


def neighbours(extended, face_set):
    up_face, down_face, left_face, right_face = face_set
    middle = extended[..., 1:-1, :]
    widths = [(0, 0)] * (middle.ndim - 1) + [(1, 1)]
    padded = jnp.pad(middle, widths)
    return (up_face * extended[..., :-2, :] + down_face * extended[..., 2:, :]
            + left_face * padded[..., :-2] + right_face * padded[..., 2:])


def relax_sweep(extended, spectrum, face_set, inverse_real, inverse_imag):
    combined = spectrum + neighbours(extended, face_set)
    update_real = inverse_real * combined[0] - inverse_imag * combined[1]
    update_imag = inverse_real * combined[1] + inverse_imag * combined[0]
    return (1.0 - OMEGA) * extended[:, 1:-1] + OMEGA * jnp.stack([update_real, update_imag])


def shifted_inverse(frequency, total_steps, diagonal_sum):
    root_alpha = jnp.power(jnp.float32(ALPHA), jnp.float32(1.0) / total_steps)
    phase_angle = 2.0 * jnp.pi * frequency.astype(jnp.float32) / total_steps
    shift_real = 1.0 - root_alpha * jnp.cos(phase_angle)
    shift_imag = root_alpha * jnp.sin(phase_angle)
    shifted = shift_real + diagonal_sum
    magnitude = shifted * shifted + shift_imag * shift_imag
    return shifted / magnitude, -shift_imag / magnitude


def dft_tables(total_steps):
    index_row = jnp.arange(total_steps, dtype=jnp.int32)
    product = (index_row[:, None] * index_row[None, :]) % total_steps
    phase_table = 2.0 * jnp.pi * product.astype(jnp.float32) / total_steps
    return jnp.cos(phase_table), jnp.sin(phase_table)


def reference(iterate, source, conduct):
    total_steps = iterate.shape[0]
    face_set = face_terms(jnp.pad(conduct, ((1, 1), (0, 0))))
    diagonal_sum = face_set[0] + face_set[1] + face_set[2] + face_set[3]
    extended = jnp.pad(iterate, ((0, 0), (1, 1), (0, 0)))
    applied = neighbours(extended, face_set) - diagonal_sum * iterate
    previous = jnp.concatenate([jnp.zeros_like(iterate[:1]), iterate[:-1]], axis=0)
    residual = source - iterate + previous + applied
    weighting = jnp.power(jnp.float32(ALPHA), jnp.arange(total_steps, dtype=jnp.int32).astype(jnp.float32) / total_steps)
    scaled = residual * weighting[:, None, None]
    cosine_table, sine_table = dft_tables(total_steps)
    highest = lax.Precision.HIGHEST
    spec_real = jnp.einsum("jn,nrc->jrc", cosine_table, scaled, precision=highest)
    spec_imag = -jnp.einsum("jn,nrc->jrc", sine_table, scaled, precision=highest)

    def solve_one(entry_pack):
        part_real, part_imag, frequency = entry_pack
        inverse_real, inverse_imag = shifted_inverse(frequency, total_steps, diagonal_sum)
        spectrum = jnp.stack([part_real, part_imag])
        solved = jnp.zeros_like(spectrum)
        for sweep_idx in range(SWEEPS):
            solved = relax_sweep(jnp.pad(solved, ((0, 0), (1, 1), (0, 0))), spectrum, face_set, inverse_real, inverse_imag)
        return solved

    solved = lax.map(solve_one, (spec_real, spec_imag, jnp.arange(total_steps, dtype=jnp.int32)))
    inverse = (jnp.einsum("nj,jrc->nrc", cosine_table, solved[:, 0], precision=highest)
               - jnp.einsum("nj,jrc->nrc", sine_table, solved[:, 1], precision=highest))
    correction = inverse / total_steps / weighting[:, None, None]
    return iterate + correction
```

```python
import functools

import jax
import jax.numpy as jnp
from jax import lax
from jax.experimental import pallas as pl
from jax.experimental.pallas import tpu as pltpu
from jax.sharding import PartitionSpec as P

ALPHA = 0.05
OMEGA = 0.8
SWEEPS = 8
LANES = 128
RIM = 8
MESH = pl.DeviceIdType.MESH
F32 = jnp.float32


def lane_index(shape):
    return lax.broadcasted_iota(jnp.int32, shape, len(shape) - 1)


def beside(own, other):
    lane = lane_index(own.shape)
    axis = own.ndim - 1
    left = jnp.where(lane == 0, pltpu.roll(other, 1, axis), pltpu.roll(own, 1, axis))
    right = jnp.where(
        lane == LANES - 1, pltpu.roll(other, LANES - 1, axis), pltpu.roll(own, LANES - 1, axis)
    )
    return left, right


def flag(condition):
    return jnp.where(condition, 1.0, 0.0).astype(F32)


def kernel(
    T, S, Z, R,
    u_hbm, s_hbm, c_hbm, out_hbm,
    u, s, c,
    edge_out, edge_in, rim_out, rim_in,
    from_prev, from_next, stage,
    xa, xb, wa, wb, qa, qb,
    pack, pack_left, pack_right,
    ca, cb, ka, kb,
    load_sem, edge_send, edge_recv, rim_send, rim_recv,
    up_send, down_send, prev_recv, next_recv,
    fwd_send, fwd_recv, row_send, row_recv, col_send, col_recv,
    back_send, back_recv,
):
    n, sp = lax.axis_index("tm"), lax.axis_index("space")
    XL = T // Z
    half = Z // 2
    z = lax.rem(n, Z)
    nxt, prv = lax.rem(n + 1, T), lax.rem(n + T - 1, T)
    below, above = lax.rem(sp + 1, S), lax.rem(sp + S - 1, S)
    has_above, has_below = flag(sp > 0), flag(sp < S - 1)
    E = R + 2 * RIM
    base = RIM
    own = base + RIM

    loads = [
        pltpu.make_async_copy(a, b, load_sem.at[i])
        for i, (a, b) in enumerate(((u_hbm, u), (c_hbm, c), (s_hbm, s)))
    ]
    for load in loads:
        load.start()

    barrier = pltpu.get_barrier_semaphore()

    def greet(i, carry):
        pl.semaphore_signal(
            barrier, inc=1, device_id=(lax.rem(n + i, T), sp), device_id_type=MESH
        )
        return carry

    lax.fori_loop(1, T, greet, 0)
    for row in (above, below):
        for step in (prv, n, nxt):
            pl.semaphore_signal(barrier, inc=1, device_id=(step, row), device_id_type=MESH)
    loads[0].wait()
    loads[1].wait()
    for side, row in ((0, 0), (1, R - 1)):
        edge_out[side, 0:1, :] = u[row : row + 1, :]
        edge_out[side, 1:2, :] = c[row : row + 1, :]
    tiles = [pl.ds(pl.multiple_of(k * LANES, LANES), LANES) for k in (prv, n, nxt)]
    for place, tile in enumerate(tiles):
        rim_out[0, place] = c[0:RIM, tile]
        rim_out[1, place] = c[R - RIM : R, tile]
    pl.semaphore_wait(barrier, T - 1 + 6)

    sides = []
    for side, row in ((0, above), (1, below)):
        for src, dst, send, recv in (
            (edge_out, edge_in, edge_send, edge_recv),
            (rim_out, rim_in, rim_send, rim_recv),
        ):
            sides.append(
                pltpu.make_async_remote_copy(
                    src_ref=src.at[side],
                    dst_ref=dst.at[1 - side],
                    send_sem=send.at[side],
                    recv_sem=recv.at[1 - side],
                    device_id=(n, row),
                    device_id_type=MESH,
                )
            )
    for copy in sides:
        copy.start()

    def columns(k):
        return pl.ds(pl.multiple_of(k * LANES, LANES), LANES)

    def place(j):
        return half - 1 - j // XL, lax.rem(j, XL)

    def block_ahead(j, start):
        away, row = place(j)
        return row * Z + lax.rem(start + away, Z)

    def block_behind(j, start):
        away, row = place(j)
        return row * Z + lax.rem(start + Z - away, Z)

    def iterate_copy(j):
        return pltpu.make_async_remote_copy(
            src_ref=u.at[:, columns(block_ahead(j, lax.rem(z + 1, Z)))],
            dst_ref=from_prev.at[j],
            send_sem=up_send,
            recv_sem=prev_recv.at[j],
            device_id=(nxt, sp),
            device_id_type=MESH,
        )

    def partial_copy(j):
        return pltpu.make_async_remote_copy(
            src_ref=stage.at[j],
            dst_ref=from_next.at[j],
            send_sem=down_send,
            recv_sem=next_recv.at[j],
            device_id=(prv, sp),
            device_id_type=MESH,
        )

    def send_iterate(j, carry):
        iterate_copy(j).start()
        return carry

    lax.fori_loop(0, T // 2, send_iterate, 0)

    loads[2].wait()
    for copy in sides[0::2]:
        copy.wait_recv()

    row_of = lax.broadcasted_iota(jnp.int32, (R, LANES), 0)

    def partial(k):
        here = columns(k)
        before, after = columns(lax.rem(k + T - 1, T)), columns(lax.rem(k + 1, T))
        inner_left, inner_right = flag(k > 0), flag(k < T - 1)
        lane = lane_index((R, LANES))

        def around(ref, which):
            middle = ref[:, here]
            left = jnp.where(
                lane == 0,
                pltpu.roll(ref[:, before], 1, 1) * inner_left,
                pltpu.roll(middle, 1, 1),
            )
            right = jnp.where(
                lane == LANES - 1,
                pltpu.roll(ref[:, after], LANES - 1, 1) * inner_right,
                pltpu.roll(middle, LANES - 1, 1),
            )
            top = edge_in[0, which : which + 1, here] * has_above
            bottom = edge_in[1, which : which + 1, here] * has_below
            up = jnp.where(row_of == 0, top, pltpu.roll(middle, 1, 0))
            down = jnp.where(row_of == R - 1, bottom, pltpu.roll(middle, R - 1, 0))
            return middle, (up, down, left, right)

        value, value_near = around(u, 0)
        cond, cond_near = around(c, 1)
        total = s[:, here] - value
        for near_value, near_cond in zip(value_near, cond_near):
            total = total + 0.5 * (cond + near_cond) * (near_value - value)
        return total

    def send_partial(j, carry):
        stage[j] = partial(block_behind(j, lax.rem(z + Z - 1, Z)))
        partial_copy(j).start()
        return carry

    lax.fori_loop(0, T // 2, send_partial, 0)

    def forward_copy(src, step, k):
        return pltpu.make_async_remote_copy(
            src_ref=src,
            dst_ref=xa.at[step, pl.ds(own, R), :],
            send_sem=fwd_send,
            recv_sem=fwd_recv.at[step],
            device_id=(k, sp),
            device_id_type=MESH,
        )

    def forward(src, step, k):
        @pl.when(k != n)
        def _():
            forward_copy(src, step, k).start()

        @pl.when(k == n)
        def _():
            pltpu.make_async_copy(
                src, xa.at[step, pl.ds(own, R), :], fwd_recv.at[step]
            ).start()

    is_first, is_last = flag(n > 0), flag(n < T - 1)

    def send_residuals(j, carry):
        partial_copy(j).wait_recv()
        k = block_behind(j, z)
        from_next[j] = from_next[j] + u[:, columns(k)] * is_last
        forward(from_next.at[j], nxt, k)
        iterate_copy(j).wait_recv()
        k = block_ahead(j, z)
        from_prev[j] = from_prev[j] * is_first + partial(k)
        forward(from_prev.at[j], n, k)
        return carry

    lax.fori_loop(0, T // 2, send_residuals, 0)

    for copy in sides[1::2]:
        copy.wait_recv()
    lane_e = lane_index((E, LANES))
    right_of, left_of = flag(n < T - 1), flag(n > 0)

    def tile_b(left, right):
        narrow = lane_index(left.shape)
        return jnp.where(narrow < LANES // 2, right * right_of, left * left_of)

    for ref, pick in (
        (ca, lambda parts: parts[1]),
        (cb, lambda parts: tile_b(parts[0], parts[2])),
    ):
        ref[base : base + RIM, :] = pick([rim_in[0, i] for i in range(3)]) * has_above
        ref[own : own + R, :] = pick([c[:, tile] for tile in tiles])
        ref[own + R : own + R + RIM, :] = pick([rim_in[1, i] for i in range(3)]) * has_below

    grid_row = sp * R - RIM + lax.broadcasted_iota(jnp.int32, (E, LANES), 0)
    row_ok = jnp.where(grid_row >= 0, 1.0, 0.0) * jnp.where(grid_row < S * R, 1.0, 0.0)
    col_ok = jnp.where(lane_e < LANES // 2, right_of, left_of)
    for ref, other, out, ok in ((ca, cb, ka, row_ok), (cb, ca, kb, row_ok * col_ok)):
        middle = ref[base : base + E, :]
        left, right = beside(middle, other[base : base + E, :])
        up, down = ref[base - 1 : base + E - 1, :], ref[base + 1 : base + E + 1, :]
        faces = [0.5 * (middle + near) for near in (up, down, left, right)]
        g = 1.0 / (1.0 + (faces[0] + faces[1] + faces[2] + faces[3]))
        for i, face in enumerate(faces):
            out[i] = jnp.where(ok > 0.0, OMEGA * g * face, 0.0)
        out[4] = g
        power = g
        count = 1
        while count < T:
            power = power * power
            count *= 2
        out[5] = ALPHA / (1.0 - ALPHA * power)
        out[6] = jnp.where(ok > 0.0, OMEGA * g, 0.0)

    def wait_forward(step, carry):
        forward_copy(xa.at[step, pl.ds(own, R), :], step, nxt).wait_recv()
        return carry

    lax.fori_loop(0, T, wait_forward, 0)

    row_copies = []
    for side, src, dst, row in (
        (0, own, own + R, above),
        (1, own + R - RIM, base, below),
    ):
        row_copies.append(
            pltpu.make_async_remote_copy(
                src_ref=xa.at[:, pl.ds(src, RIM), :],
                dst_ref=xa.at[:, pl.ds(dst, RIM), :],
                send_sem=row_send.at[side],
                recv_sem=row_recv.at[1 - side],
                device_id=(n, row),
                device_id_type=MESH,
            )
        )
    for copy in row_copies:
        copy.start()

    GROUPS = T // 8
    RG = R // 8
    lane_8 = lane_index((8, LANES))

    def pack_group(group, carry):
        for i in range(RG):
            total = jnp.zeros((8, LANES), F32)
            for j in range(8):
                rolled = pltpu.roll(xa[group * 8 + j, own + 8 * i : own + 8 * i + 8, :], 16 * j + 8, 1)
                total = jnp.where(lane_8 // 16 == j, rolled, total)
            pack[i, group] = total
        return carry

    lax.fori_loop(0, GROUPS, pack_group, 0)

    col_copies = []
    for side, (ref, step) in enumerate(((pack_left, nxt), (pack_right, prv))):
        for part, (src, dst, row) in enumerate((
            (pack, ref.at[pl.ds(1, RG)], sp),
            (pack.at[pl.ds(0, 1)], ref.at[pl.ds(RG + 1, 1)], above),
            (pack.at[pl.ds(RG - 1, 1)], ref.at[pl.ds(0, 1)], below),
        )):
            col_copies.append(
                pltpu.make_async_remote_copy(
                    src_ref=src,
                    dst_ref=dst,
                    send_sem=col_send.at[side * 3 + part],
                    recv_sem=col_recv.at[side * 3 + part],
                    device_id=(step, row),
                    device_id_type=MESH,
                )
            )
    for copy in col_copies:
        copy.start()
    for copy in col_copies:
        copy.wait_recv()

    def unpack_group(group, carry):
        for i in range(RG + 2):
            merged = jnp.where(
                lax.rem(lane_8, 16) < 8, pack_left[i, group], pack_right[i, group]
            )
            for j in range(8):
                xb[group * 8 + j, base + 8 * i : base + 8 * i + 8, :] = pltpu.roll(
                    merged, LANES - 8 - 16 * j, 1
                )
        return carry

    lax.fori_loop(0, GROUPS, unpack_group, 0)
    for copy in row_copies:
        copy.wait()

    BLOCK = 16
    UNROLL = 8

    def over_time(body, carry):
        def step(i, carry):
            for j in range(UNROLL):
                carry = body(i * UNROLL + j, carry)
            return carry

        return lax.fori_loop(0, T // UNROLL, step, carry)

    zero = jnp.zeros((BLOCK, LANES), F32)

    def wrap(first, dsts, coeffs, last):
        rows = pl.ds(base + first, BLOCK)
        gains = [k[4, first : first + BLOCK, :] for k in coeffs]
        start = tuple(
            value * k[5, first : first + BLOCK, :] for value, k in zip(last, coeffs)
        )

        def body(t, carry):
            new = []
            for dst, gain, value in zip(dsts, gains, carry):
                value = gain * value
                dst[t, rows, :] = dst[t, rows, :] + value
                new.append(value)
            return tuple(new)

        over_time(body, start)

    def first_sweep(first):
        rows = pl.ds(base + first, BLOCK)
        q_rows = pl.ds(first, BLOCK)
        for x, w, q, k in ((xa, wa, qa, ka), (xb, wb, qb, kb)):
            gain, weight = k[4, first : first + BLOCK, :], k[6, first : first + BLOCK, :]
            ok = weight > 0.0

            def body(t, carry):
                scaled = jnp.where(ok, weight * x[t, rows, :], 0.0)
                q[t, q_rows, :] = scaled
                value = scaled + gain * carry
                w[t, rows, :] = value
                return value

            last = over_time(body, zero)
            wrap(first, (w,), (k,), (last,))

    def sweep(first, src_a, src_b, dst_a, dst_b, both):
        rows = pl.ds(base + first, BLOCK)
        rows_up, rows_down = pl.ds(base + first - 1, BLOCK), pl.ds(base + first + 1, BLOCK)
        q_rows = pl.ds(first, BLOCK)
        kept = (ka, kb) if both else (ka,)
        coeffs = [[k[i, first : first + BLOCK, :] for i in range(5)] for k in kept]

        def body(t, carry):
            a, b = src_a[t, rows, :], src_b[t, rows, :]
            new = []
            for src, dst, q, mine, other, k, value in zip(
                (src_a, src_b), (dst_a, dst_b), (qa, qb), (a, b), (b, a), coeffs, carry
            ):
                left, right = beside(mine, other)
                near = k[0] * src[t, rows_up, :] + k[1] * src[t, rows_down, :]
                near = near + (k[2] * left + k[3] * right)
                value = (q[t, q_rows, :] + near) + k[4] * value
                dst[t, rows, :] = (1.0 - OMEGA) * mine + value
                new.append(value)
            return tuple(new)

        last = over_time(body, (zero,) * len(kept))
        wrap(first, (dst_a, dst_b)[: len(kept)], kept, last)

    for first in range(0, E, BLOCK):
        first_sweep(first)

    def two_sweeps(i, carry):
        for first in range(0, E, BLOCK):
            sweep(first, wa, wb, xa, xb, True)
        for first in range(0, E, BLOCK):
            sweep(first, xa, xb, wa, wb, True)
        return carry

    lax.fori_loop(0, (SWEEPS - 2) // 2, two_sweeps, 0)
    for first in range(RIM, RIM + R, BLOCK):
        sweep(first, wa, wb, xa, xb, False)

    def back_copy(step, block):
        return pltpu.make_async_remote_copy(
            src_ref=xa.at[step, pl.ds(own, R), :],
            dst_ref=out_hbm.at[:, columns(block)],
            send_sem=back_send,
            recv_sem=back_recv.at[block],
            device_id=(step, sp),
            device_id_type=MESH,
        )

    def send_back(j, carry):
        m = j // XL
        away = half - (m + 1) // 2
        toward = jnp.where(lax.rem(m, 2) == 1, away, Z - away)
        step = lax.rem(j, XL) * Z + lax.rem(z + toward, Z)

        @pl.when(step != n)
        def _():
            back_copy(step, n).start()

        @pl.when(step == n)
        def _():
            pltpu.make_async_copy(
                xa.at[step, pl.ds(own, R), :], out_hbm.at[:, columns(n)], back_recv.at[n]
            ).start()

        return carry

    lax.fori_loop(0, T, send_back, 0)

    for copy in sides:
        copy.wait_send()
    for copy in col_copies:
        copy.wait_send()
    pltpu.make_async_copy(from_prev, from_prev, up_send).wait()
    pltpu.make_async_copy(stage, stage, down_send).wait()
    sent = xa.at[pl.ds(0, T - 2), pl.ds(own, R), :]
    pltpu.make_async_copy(sent, sent, fwd_send).wait()
    sent = xa.at[pl.ds(0, T - 1), pl.ds(own, R), :]
    pltpu.make_async_copy(sent, sent, back_send).wait()

    def wait_back(block, carry):
        back_copy(nxt, block).wait_recv()
        return carry

    lax.fori_loop(0, T, wait_back, 0)


def per_device(iterate, source, conduct):
    T, S = lax.axis_size("tm"), lax.axis_size("space")
    R, NC = conduct.shape
    Z = T // 2
    E = R + 2 * RIM
    padded = E + 16
    dma = pltpu.SemaphoreType.DMA
    vmem = lambda *shape: pltpu.VMEM(shape, F32)
    any_space = pl.BlockSpec(memory_space=pl.ANY)
    correction = pl.pallas_call(
        functools.partial(kernel, T, S, Z, R),
        out_shape=jax.ShapeDtypeStruct((R, NC), F32),
        in_specs=[any_space] * 3,
        out_specs=any_space,
        scratch_shapes=[
            vmem(R, NC), vmem(R, NC), vmem(R, NC),
            vmem(2, 2, NC), vmem(2, 2, NC), vmem(2, 3, RIM, LANES), vmem(2, 3, RIM, LANES),
            vmem(T // 2, R, LANES), vmem(T // 2, R, LANES), vmem(T // 2, R, LANES),
            vmem(T, padded, LANES), vmem(T, padded, LANES),
            vmem(T, padded, LANES), vmem(T, padded, LANES),
            vmem(T, E, LANES), vmem(T, E, LANES),
            vmem(R // 8, T // 8, 8, LANES),
            vmem(R // 8 + 2, T // 8, 8, LANES), vmem(R // 8 + 2, T // 8, 8, LANES),
            vmem(padded, LANES), vmem(padded, LANES),
            vmem(7, E, LANES), vmem(7, E, LANES),
            dma((3,)), dma((2,)), dma((2,)), dma((2,)), dma((2,)),
            dma, dma, dma((T // 2,)), dma((T // 2,)),
            dma, dma((T,)), dma((2,)), dma((2,)), dma((6,)), dma((6,)),
            dma, dma((T,)),
        ],
        compiler_params=pltpu.CompilerParams(
            collective_id=0, has_side_effects=True, vmem_limit_bytes=32 * 1024 * 1024
        ),
    )(iterate[0], source[0], conduct)
    return iterate + correction[None]


def solution(mesh):
    return jax.shard_map(
        per_device,
        mesh=mesh,
        in_specs=(P("tm", "space", None), P("tm", "space", None), P("space", None)),
        out_specs=P("tm", "space", None),
        check_vma=False,
    )
```

```python
import functools

import jax
import jax.numpy as jnp
from jax import lax
from jax.experimental import pallas as pl
from jax.experimental.pallas import tpu as pltpu
from jax.sharding import PartitionSpec as P

ALPHA = 0.05
OMEGA = 0.8
SWEEPS = 8
LANES = 128
WIDTH = 64
RIM = 8
MESH = pl.DeviceIdType.MESH
F32 = jnp.float32


def lane_index(shape):
    return lax.broadcasted_iota(jnp.int32, shape, len(shape) - 1)


def roll(value, shift):
    shift = shift % LANES
    return pltpu.roll(value, shift, value.ndim - 1) if shift else value


def flag(condition):
    return jnp.where(condition, 1.0, 0.0).astype(F32)


def kernel(
    T, S, Z, R,
    u_hbm, s_hbm, c_hbm, out_hbm,
    u, s, c, out,
    edge_out, edge_in, rim_out, rim_in,
    u_stage, s_stage, from_prev, from_next,
    gathered, rows_out, rows_in, right_out, left_out, right_in, left_in,
    x_buf, w_buf, q_buf, cond_buf, coeff,
    back_out, back_in,
    load_sem, store_sem, edge_send, edge_recv, rim_send, rim_recv,
    u_send, s_send, prev_recv, next_recv,
    fwd_send, fwd_recv, row_send, row_recv, col_send, col_recv,
    back_send, back_recv,
):
    n, sp = lax.axis_index("tm"), lax.axis_index("space")
    XL = T // Z
    half = Z // 2
    z = lax.rem(n, Z)
    z_next, z_prev = lax.rem(z + 1, Z), lax.rem(z + Z - 1, Z)
    nxt, prv = lax.rem(n + 1, T), lax.rem(n + T - 1, T)
    below, above = lax.rem(sp + 1, S), lax.rem(sp + S - 1, S)
    has_above, has_below = flag(sp > 0), flag(sp < S - 1)
    H = R // 2
    E = R + 2 * RIM
    base = RIM
    own = base + RIM
    PAIRS = T // 2

    finish = []
    loads = []
    pieces = [(0, RIM), (R - RIM, RIM), (RIM, R - 2 * RIM)]
    for i, (a, b) in enumerate(((u_hbm, u), (c_hbm, c), (s_hbm, s))):
        loads.append([
            pltpu.make_async_copy(a.at[pl.ds(at, rows)], b.at[pl.ds(at, rows)], load_sem.at[i, q])
            for q, (at, rows) in enumerate(pieces)
        ])
    for group in ((0, 0), (0, 1), (1, 0), (1, 1), (0, 2), (1, 2), (2, 0), (2, 1), (2, 2)):
        loads[group[0]][group[1]].start()

    barrier = pltpu.get_barrier_semaphore()

    def greet(i, carry):
        pl.semaphore_signal(
            barrier, inc=1, device_id=(lax.rem(n + i, T), sp), device_id_type=MESH
        )
        return carry

    lax.fori_loop(1, T, greet, 0)
    for row in (above, below):
        pl.semaphore_signal(barrier, inc=1, device_id=(n, row), device_id_type=MESH)

    def columns(tile):
        return pl.ds(pl.multiple_of(tile * LANES, LANES), LANES)

    def remote(src, dst, send, recv, step, row):
        return pltpu.make_async_remote_copy(
            src_ref=src, dst_ref=dst, send_sem=send, recv_sem=recv,
            device_id=(step, row), device_id_type=MESH,
        )

    def pack(low, high, odd):
        lane = lane_index(low.shape)
        is_odd = jnp.zeros(low.shape, jnp.int32) + odd
        kept = jnp.where(is_odd == 1, high, low)
        moved = roll(jnp.where(is_odd == 1, low, high), WIDTH)
        return jnp.where(lane // WIDTH == is_odd, kept, moved)

    def conduct_tile(rows, half_index):
        block = half_index * T + n
        tile, odd = block // 2, lax.rem(block, 2)
        first = c[rows, columns(lax.rem(tile + odd, T))]
        second = c[rows, columns(lax.rem(tile + odd + T - 1, T))]
        lane = lane_index(first.shape)
        is_odd = jnp.zeros(first.shape, jnp.int32) + odd
        joined = jnp.where(lane < 96 - WIDTH * is_odd, first, second)
        placed = jnp.where(is_odd == 1, roll(joined, WIDTH), joined)
        right_ok, left_ok = flag(block < 2 * T - 1), flag(block > 0)
        keep = jnp.where(lane < WIDTH, 1.0, jnp.where(lane < 96, right_ok, left_ok))
        return jnp.where(keep > 0.0, placed, 0.0)

    for i, q in ((0, 0), (0, 1), (1, 0), (1, 1)):
        loads[i][q].wait()
    for side, row, rows in ((0, 0, slice(0, RIM)), (1, R - 1, slice(R - RIM, R))):
        edge_out[side, 0:1, :] = u[row : row + 1, :]
        edge_out[side, 1:2, :] = c[row : row + 1, :]
        for p in range(2):
            rim_out[side, p] = conduct_tile(rows, p)
    loads[0][2].wait()
    loads[1][2].wait()
    pl.semaphore_wait(barrier, T - 1 + 2)

    sides = []
    for src, dst, send, recv in (
        (edge_out, edge_in, edge_send, edge_recv),
        (rim_out, rim_in, rim_send, rim_recv),
    ):
        for side, row in ((0, above), (1, below)):
            sides.append(
                remote(src.at[side], dst.at[1 - side], send.at[side], recv.at[1 - side], n, row)
            )
    for copy in sides:
        copy.start()
        finish.append(copy.wait_send)

    def owner_ahead(j, start):
        away = half - 1 - j // XL
        return lax.rem(j, XL) * Z + lax.rem(start + away, Z)

    def owner_behind(j, start):
        away = half - 1 - j // XL
        return lax.rem(j, XL) * Z + lax.rem(start + Z - away, Z)

    def u_copy(p, j):
        return remote(
            u_stage.at[p, j], from_prev.at[p, j], u_send, prev_recv.at[p, j], nxt, sp
        )

    def s_copy(p, j):
        return remote(
            s_stage.at[p, j], from_next.at[p, j], s_send, next_recv.at[p, j], prv, sp
        )

    row_of = lax.broadcasted_iota(jnp.int32, (R, LANES), 0)
    lane_r = lane_index((R, LANES))

    def packed_iterate(p, k):
        here = columns((p * T + k) // 2)
        return pack(u[0:H, here], u[H:R, here], lax.rem(k, 2))

    def packed_partial(p, k):
        tile = (p * T + k) // 2
        here = columns(tile)
        before, after = columns(lax.rem(tile + T - 1, T)), columns(lax.rem(tile + 1, T))
        inner_left, inner_right = flag(tile > 0), flag(tile < T - 1)

        def around(ref, which):
            middle = ref[:, here]
            left = jnp.where(lane_r == 0, roll(ref[:, before], 1) * inner_left, roll(middle, 1))
            right = jnp.where(
                lane_r == LANES - 1, roll(ref[:, after], -1) * inner_right, roll(middle, -1)
            )
            top = edge_in[0, which : which + 1, here] * has_above
            bottom = edge_in[1, which : which + 1, here] * has_below
            up = jnp.where(row_of == 0, top, pltpu.roll(middle, 1, 0))
            down = jnp.where(row_of == R - 1, bottom, pltpu.roll(middle, R - 1, 0))
            return middle, (up, down, left, right)

        value, value_near = around(u, 0)
        cond, cond_near = around(c, 1)
        total = s[:, here] - value
        for near_value, near_cond in zip(value_near, cond_near):
            total = total + 0.5 * (cond + near_cond) * (near_value - value)
        return pack(total[0:H], total[H:R], lax.rem(k, 2))

    def over_blocks(p, owner, start, send):
        def step(j, carry):
            if p == 0:
                send(0, j, owner(j, start))
            else:
                k = owner(j, start)
                pl.when(k != 0)(lambda: send(1, j, k))
            return carry

        def early(j, carry):
            k = owner(j, start)
            pl.when(k == 0)(lambda: send(1, j, k))
            return carry

        if p == 0:
            lax.fori_loop(0, PAIRS, early, 0)
        lax.fori_loop(0, PAIRS, step, 0)

    def send_iterate(p, j, k):
        u_stage[p, j] = packed_iterate(p, k)
        u_copy(p, j).start()

    def send_partial(p, j, k):
        s_stage[p, j] = packed_partial(p, k)
        s_copy(p, j).start()

    over_blocks(0, owner_ahead, z_next, send_iterate)
    for load in loads[2]:
        load.wait()
    for copy in sides[0:2]:
        copy.wait_recv()
    over_blocks(0, owner_behind, z_prev, send_partial)
    finish.append(pltpu.make_async_copy(u_stage, u_stage, u_send).wait)
    finish.append(pltpu.make_async_copy(s_stage, s_stage, s_send).wait)

    def forward_copy(src, p, step, k):
        return remote(src, gathered.at[p, step], fwd_send, fwd_recv.at[p, step], k, sp)

    def forward(src, p, step, k):
        @pl.when(k != n)
        def _():
            forward_copy(src, p, step, k).start()

        @pl.when(k == n)
        def _():
            pltpu.make_async_copy(src, gathered.at[p, step], fwd_recv.at[p, step]).start()

    is_first, is_last = flag(n > 0), flag(n < T - 1)

    def forward_behind(p, j, k):
        s_copy(p, j).wait_recv()
        from_next[p, j] = from_next[p, j] + packed_iterate(p, k) * is_last
        forward(from_next.at[p, j], p, nxt, k)

    def forward_ahead(p, j, k):
        u_copy(p, j).wait_recv()
        from_prev[p, j] = from_prev[p, j] * is_first + packed_partial(p, k)
        forward(from_prev.at[p, j], p, n, k)

    def forward_some(p, start, stop, only=None):
        def both(j, carry):
            for owner, send in ((owner_behind, forward_behind), (owner_ahead, forward_ahead)):
                k = owner(j, z)
                if only is None:
                    send(p, j, k)
                else:
                    pl.when((k == 0) == only)(functools.partial(send, p, j, k))
            return carry

        lax.fori_loop(start, stop, both, 0)

    forward_some(1, 0, PAIRS, only=True)
    forward_some(0, 0, PAIRS)
    over_blocks(1, owner_ahead, z_next, send_iterate)
    over_blocks(1, owner_behind, z_prev, send_partial)
    sent = gathered.at[:, pl.ds(0, T - 2)]
    finish.append(pltpu.make_async_copy(sent, sent, fwd_send).wait)

    for copy in sides[2:4]:
        copy.wait_recv()
    lane_e = lane_index((E, LANES))
    grid_row = sp * R - RIM + lax.broadcasted_iota(jnp.int32, (E, LANES), 0)
    row_ok = jnp.where(grid_row >= 0, 1.0, 0.0) * jnp.where(grid_row < S * R, 1.0, 0.0)
    for p in range(2):
        cond_buf[base : base + RIM, :] = rim_in[0, p] * has_above
        cond_buf[own : own + R, :] = conduct_tile(slice(0, R), p)
        cond_buf[own + R : own + R + RIM, :] = rim_in[1, p] * has_below
        block = p * T + n
        right_ok, left_ok = flag(block < 2 * T - 1), flag(block > 0)
        ok = row_ok * jnp.where(lane_e < WIDTH, 1.0, jnp.where(lane_e < 96, right_ok, left_ok))
        middle = cond_buf[base : base + E, :]
        up, down = cond_buf[base - 1 : base + E - 1, :], cond_buf[base + 1 : base + E + 1, :]
        faces = [0.5 * (middle + near) for near in (up, down, roll(middle, 1), roll(middle, -1))]
        g = 1.0 / (1.0 + (faces[0] + faces[1] + faces[2] + faces[3]))
        for i, face in enumerate(faces):
            coeff[p, i] = jnp.where(ok > 0.0, OMEGA * g * face, 0.0)
        coeff[p, 4] = g
        power = g
        count = 1
        while count < T:
            power = power * power
            count *= 2
        coeff[p, 5] = ALPHA / (1.0 - ALPHA * power)
        coeff[p, 6] = jnp.where(ok > 0.0, OMEGA * g, 0.0)

    lane_8 = lane_index((8, LANES))
    segment, in_first = lane_8 // 16, lax.rem(lane_8, 16) < 8
    in_low = lane_8 < WIDTH

    def row_copies(p, group):
        return [
            remote(
                rows_out.at[p, side, group], rows_in.at[p, 1 - side, group],
                row_send, row_recv.at[p, 1 - side], n, row,
            )
            for side, row in ((0, above), (1, below))
        ]

    def send_rows(p):
        def pass_rows(group, carry):
            for j in range(8):
                forward_copy(gathered.at[p, 0], p, group * 8 + j, nxt).wait_recv()
            for j in range(4):
                step = group * 8 + 2 * j
                top, top_next = gathered[p, step, 0:8], gathered[p, step + 1, 0:8]
                rows_out[p, 0, group, j] = jnp.where(in_low, top, roll(top_next, WIDTH))
                bottom = gathered[p, step, H - 8 : H]
                bottom_next = gathered[p, step + 1, H - 8 : H]
                rows_out[p, 1, group, j] = jnp.where(in_low, roll(bottom, WIDTH), bottom_next)
            for copy in row_copies(p, group):
                copy.start()
            return carry

        lax.fori_loop(0, T // 8, pass_rows, 0)

    def packed_rows(p, group, j, i):
        if i < 2:
            return gathered[p, group * 8 + j, 8 * i : 8 * i + 8]
        down, up = rows_in[p, 1, group, j // 2], rows_in[p, 0, group, j // 2]
        if j % 2:
            return jnp.where(in_low, roll(down, WIDTH), up)
        return jnp.where(in_low, down, roll(up, WIDTH))

    def pack_edges(p):
        for side in range(2):
            whole = rows_in.at[p, side]
            pltpu.make_async_copy(whole, whole, row_recv.at[p, side]).wait()

        def pack_group(group, carry):
            for i in range(3):
                first = jnp.zeros((8, LANES), F32)
                second = first
                for j in range(8):
                    value = packed_rows(p, group, j, i)
                    first = jnp.where(segment == j, roll(value, 16 * j - 56), first)
                    second = jnp.where(segment == j, roll(value, 16 * j + 8), second)
                right_out[p, i, group] = jnp.where(in_first, first, roll(second, 8))
                left_out[p, i, group] = jnp.where(in_first, roll(first, -8), second)
            return carry

        lax.fori_loop(0, T // 8, pack_group, 0)

    def columns_copies(p):
        right = right_out.at[jnp.where(n == T - 1, 0, p)]
        left = left_out.at[jnp.where(n == 0, 1, p)]
        return (
            remote(right, right_in.at[p], col_send.at[p, 0], col_recv.at[p, 0], nxt, sp),
            remote(left, left_in.at[p], col_send.at[p, 1], col_recv.at[p, 1], prv, sp),
        )

    GROUPS = ((0, 2), (1, 3), (4, -1))

    def unpack(p):
        def unpack_group(group, carry):
            for i, (low, high) in enumerate(GROUPS):
                from_left, from_right = right_in[p, i, group], left_in[p, i, group]
                for j in range(8):
                    step = group * 8 + j
                    value = packed_rows(p, group, j, i)
                    for place, own_part, left_at, right_at in (
                        (low, value, 0, 8),
                        (high, roll(value, WIDTH), 8, 0),
                    ):
                        left = roll(from_left, 120 - 16 * j - left_at)
                        right = roll(from_right, 64 - 16 * j - right_at)
                        x_buf[step, own + 8 * place : own + 8 * place + 8, :] = jnp.where(
                            in_low, own_part, jnp.where(lane_8 < 96, right, left)
                        )
            return carry

        lax.fori_loop(0, T // 8, unpack_group, 0)

    def over_time(body, carry):
        for step in range(T):
            carry = body(step, carry)
        return carry

    def wrap(p, first, rows, dst, last):
        here = pl.ds(base + first, rows)
        gain = coeff[p, 4, first : first + rows, :]

        def body(t, carry):
            carry = gain * carry
            dst[t, here, :] = dst[t, here, :] + carry
            return carry

        over_time(body, last * coeff[p, 5, first : first + rows, :])

    def first_sweep(p, first, rows, src, dst):
        here, q_here = pl.ds(base + first, rows), pl.ds(first, rows)
        gain = coeff[p, 4, first : first + rows, :]
        weight = coeff[p, 6, first : first + rows, :]
        ok = weight > 0.0

        def body(t, carry):
            scaled = jnp.where(ok, weight * src[t, here, :], 0.0)
            q_buf[t, q_here, :] = scaled
            value = scaled + gain * carry
            dst[t, here, :] = value
            return value

        last = over_time(body, jnp.zeros((rows, LANES), F32))
        wrap(p, first, rows, dst, last)

    def sweep(p, first, rows, src, dst):
        here, q_here = pl.ds(base + first, rows), pl.ds(first, rows)
        here_up, here_down = pl.ds(base + first - 1, rows), pl.ds(base + first + 1, rows)
        k = [coeff[p, i, first : first + rows, :] for i in range(5)]

        def body(t, carry):
            mine = src[t, here, :]
            near = k[0] * src[t, here_up, :] + k[1] * src[t, here_down, :]
            near = near + (k[2] * roll(mine, 1) + k[3] * roll(mine, -1))
            value = (q_buf[t, q_here, :] + near) + k[4] * carry
            dst[t, here, :] = (1.0 - OMEGA) * mine + value
            return value

        last = over_time(body, jnp.zeros((rows, LANES), F32))
        wrap(p, first, rows, dst, last)

    def blocks_of(first, stop, rows):
        return [(at, min(rows, stop - at)) for at in range(first, stop, rows)]

    BLOCK = 24

    def solve(p):
        for first, rows in blocks_of(0, E, BLOCK):
            first_sweep(p, first, rows, x_buf, w_buf)

        def two_sweeps(i, carry):
            for first, rows in blocks_of(0, E, BLOCK):
                sweep(p, first, rows, w_buf, x_buf)
            for first, rows in blocks_of(0, E, BLOCK):
                sweep(p, first, rows, x_buf, w_buf)
            return carry

        lax.fori_loop(0, (SWEEPS - 2) // 2, two_sweeps, 0)
        for first, rows in blocks_of(RIM, RIM + R, 16):
            sweep(p, first, rows, w_buf, x_buf)

    def back_copy(p, step, k):
        return remote(back_out.at[p, step], back_in.at[p, k], back_send, back_recv.at[p, k], step, sp)

    def pack_back(p):
        lane = lane_index((H, LANES))

        def pack_step(step, carry):
            low, high = x_buf[step, own : own + H, :], x_buf[step, own + H : own + R, :]
            back_out[p, step] = jnp.where(lane < WIDTH, low, roll(high, WIDTH))
            return carry

        lax.fori_loop(0, T, pack_step, 0)

    def give_back(p, start, stop):
        def send(j, carry):
            m = j // XL
            away = half - (m + 1) // 2
            toward = jnp.where(lax.rem(m, 2) == 1, away, Z - away)
            step = lax.rem(j, XL) * Z + lax.rem(z + toward, Z)

            @pl.when(step != n)
            def _():
                back_copy(p, step, n).start()

            @pl.when(step == n)
            def _():
                pltpu.make_async_copy(
                    back_out.at[p, step], back_in.at[p, n], back_recv.at[p, n]
                ).start()

            return carry

        lax.fori_loop(start, stop, send, 0)

    def store_copy(tile):
        return pltpu.make_async_copy(out.at[:, columns(tile)], out_hbm.at[:, columns(tile)], store_sem)

    def update(p):
        lane = lane_index((H, LANES))

        def step(j, carry):
            m = j // XL
            away = half // 2 - (m + 1) // 2
            toward = jnp.where(lax.rem(m, 2) == 1, away, half - away)
            pair = lax.rem(j, XL) * half + lax.rem(z // 2 + toward, half)
            for k in (2 * pair, 2 * pair + 1):
                back_copy(p, nxt, k).wait_recv()
            even, odd = back_in[p, 2 * pair], back_in[p, 2 * pair + 1]
            tile = p * PAIRS + pair
            here = columns(tile)
            out[0:H, here] = u[0:H, here] + jnp.where(lane < WIDTH, even, roll(odd, WIDTH))
            out[H:R, here] = u[H:R, here] + jnp.where(lane < WIDTH, roll(even, WIDTH), odd)
            store_copy(tile).start()
            return carry

        lax.fori_loop(0, PAIRS, step, 0)

    def pass_columns(p):
        copies = columns_copies(p)
        for copy in copies:
            copy.start()
            finish.append(copy.wait_send)
        return copies

    send_rows(0)
    pl.when(n == 0)(lambda: send_rows(1))
    forward_some(1, 0, PAIRS // 2, only=False)
    pack_edges(0)
    pl.when(n == 0)(lambda: pack_edges(1))
    first_columns = pass_columns(0)
    forward_some(1, PAIRS // 2, PAIRS, only=False)
    for copy in first_columns:
        copy.wait_recv()
    unpack(0)
    solve(0)
    pack_back(0)

    pl.when(n != 0)(lambda: send_rows(1))
    give_back(0, 0, T // 4)
    pl.when(n != 0)(lambda: pack_edges(1))
    second_columns = pass_columns(1)
    give_back(0, T // 4, T // 2)
    for copy in second_columns:
        copy.wait_recv()
    unpack(1)
    give_back(0, T // 2, T)
    solve(1)
    pack_back(1)
    give_back(1, 0, T)
    update(0)
    update(1)
    whole = rows_in
    finish.append(pltpu.make_async_copy(whole, whole, row_send).wait)
    sent = back_out.at[:, pl.ds(0, T - 1)]
    finish.append(pltpu.make_async_copy(sent, sent, back_send).wait)
    finish.append(pltpu.make_async_copy(out, out, store_sem).wait)
    for wait in finish:
        wait()


def per_device(iterate, source, conduct):
    T, S = lax.axis_size("tm"), lax.axis_size("space")
    R, NC = conduct.shape
    Z = T // 2
    E = R + 2 * RIM
    dma = pltpu.SemaphoreType.DMA
    vmem = lambda *shape: pltpu.VMEM(shape, F32)
    block = (R // 2, LANES)
    group = (T // 8, 8, LANES)
    in_hbm = pl.BlockSpec(memory_space=pltpu.HBM)
    updated = pl.pallas_call(
        functools.partial(kernel, T, S, Z, R),
        out_shape=jax.ShapeDtypeStruct((R, NC), F32),
        in_specs=[in_hbm] * 3,
        out_specs=in_hbm,
        scratch_shapes=[
            vmem(R, NC), vmem(R, NC), vmem(R, NC), vmem(R, NC),
            vmem(2, 2, NC), vmem(2, 2, NC), vmem(2, 2, RIM, LANES), vmem(2, 2, RIM, LANES),
            vmem(2, T // 2, *block), vmem(2, T // 2, *block),
            vmem(2, T // 2, *block), vmem(2, T // 2, *block),
            vmem(2, T, *block), vmem(2, 2, T // 8, 4, RIM, LANES), vmem(2, 2, T // 8, 4, RIM, LANES),
            vmem(2, 3, *group), vmem(2, 3, *group), vmem(2, 3, *group), vmem(2, 3, *group),
            vmem(T, E + 16, LANES), vmem(T, E + 16, LANES), vmem(T, E, LANES),
            vmem(E + 16, LANES), vmem(2, 7, E, LANES),
            vmem(2, T, *block), vmem(2, T, *block),
            dma((3, 3)), dma, dma((2,)), dma((2,)), dma((2,)), dma((2,)),
            dma, dma, dma((2, T // 2)), dma((2, T // 2)),
            dma, dma((2, T)), dma, dma((2, 2)), dma((2, 2)), dma((2, 2)),
            dma, dma((2, T)),
        ],
        compiler_params=pltpu.CompilerParams(
            collective_id=0, has_side_effects=True, vmem_limit_bytes=60 * 1024 * 1024
        ),
    )(iterate[0], source[0], conduct)
    return updated[None]


def solution(mesh):
    return jax.shard_map(
        per_device,
        mesh=mesh,
        in_specs=(P("tm", "space", None), P("tm", "space", None), P("space", None)),
        out_specs=P("tm", "space", None),
        check_vma=False,
    )
```

```python
import functools

import jax
import jax.numpy as jnp
from jax import lax
from jax.experimental import pallas as pl
from jax.experimental.pallas import tpu as pltpu
from jax.sharding import PartitionSpec as P

ALPHA = 0.05
OMEGA = 0.8
SWEEPS = 8
LANES = 128
WIDTH = 64
RIM = 8
MESH = pl.DeviceIdType.MESH
F32 = jnp.float32


def lane_index(shape):
    return lax.broadcasted_iota(jnp.int32, shape, len(shape) - 1)


def roll(value, shift):
    shift = shift % LANES
    return pltpu.roll(value, shift, value.ndim - 1) if shift else value


def flag(condition):
    return jnp.where(condition, 1.0, 0.0).astype(F32)


def kernel(
    T, S, Z, R,
    u_hbm, s_hbm, c_hbm, out_hbm,
    u, s, c, out, part,
    edge_out, edge_in, rim_out, rim_in,
    u_stage, s_stage, from_prev, from_next,
    gathered, rows_out, rows_in, right_out, left_out, right_in, left_in,
    x_buf, w_buf, q_buf, cond_buf, coeff,
    back_out, back_in,
    load_sem, store_sem, edge_send, edge_recv, rim_send, rim_recv,
    u_send, s_send, prev_recv, next_recv,
    fwd_send, fwd_recv, halo_send, row_recv, col_send, col_recv, corner_recv,
    back_send, back_recv,
):
    n, sp = lax.axis_index("tm"), lax.axis_index("space")
    XL = T // Z
    half = Z // 2
    z = lax.rem(n, Z)
    z_next, z_prev = lax.rem(z + 1, Z), lax.rem(z + Z - 1, Z)
    nxt, prv = lax.rem(n + 1, T), lax.rem(n + T - 1, T)
    below, above = lax.rem(sp + 1, S), lax.rem(sp + S - 1, S)
    has_above, has_below = flag(sp > 0), flag(sp < S - 1)
    H = R // 2
    E = R + 2 * RIM
    base = RIM
    own = base + RIM
    PAIRS = T // 2
    PIECES = 4
    PIECE = PAIRS // PIECES

    finish = []
    loads = []
    pieces = [(0, RIM), (R - RIM, RIM), (RIM, R - 2 * RIM)]
    for i, (a, b) in enumerate(((u_hbm, u), (c_hbm, c), (s_hbm, s))):
        loads.append([
            pltpu.make_async_copy(a.at[pl.ds(at, rows)], b.at[pl.ds(at, rows)], load_sem.at[i, q])
            for q, (at, rows) in enumerate(pieces)
        ])
    for group in ((0, 0), (0, 1), (1, 0), (1, 1), (0, 2), (1, 2), (2, 0), (2, 1), (2, 2)):
        loads[group[0]][group[1]].start()

    barrier = pltpu.get_barrier_semaphore()

    def greet(i, carry):
        pl.semaphore_signal(
            barrier, inc=1, device_id=(lax.rem(n + i, T), sp), device_id_type=MESH
        )
        return carry

    lax.fori_loop(1, T, greet, 0)
    there = ((sp > 0, above), (sp < S - 1, below))
    for exists, row in there:
        @pl.when(exists)
        def _(row=row):
            for step in (prv, n, nxt):
                pl.semaphore_signal(barrier, inc=1, device_id=(step, row), device_id_type=MESH)

    def columns(tile):
        return pl.ds(pl.multiple_of(tile * LANES, LANES), LANES)

    def remote(src, dst, send, recv, step, row):
        return pltpu.make_async_remote_copy(
            src_ref=src, dst_ref=dst, send_sem=send, recv_sem=recv,
            device_id=(step, row), device_id_type=MESH,
        )

    def pack(low, high, odd):
        lane = lane_index(low.shape)
        is_odd = jnp.zeros(low.shape, jnp.int32) + odd
        kept = jnp.where(is_odd == 1, high, low)
        moved = roll(jnp.where(is_odd == 1, low, high), WIDTH)
        return jnp.where(lane // WIDTH == is_odd, kept, moved)

    def conduct_tile(rows, half_index):
        block = half_index * T + n
        tile, odd = block // 2, lax.rem(block, 2)
        first = c[rows, columns(lax.rem(tile + odd, T))]
        second = c[rows, columns(lax.rem(tile + odd + T - 1, T))]
        lane = lane_index(first.shape)
        is_odd = jnp.zeros(first.shape, jnp.int32) + odd
        joined = jnp.where(lane < 96 - WIDTH * is_odd, first, second)
        placed = jnp.where(is_odd == 1, roll(joined, WIDTH), joined)
        right_ok, left_ok = flag(block < 2 * T - 1), flag(block > 0)
        keep = jnp.where(lane < WIDTH, 1.0, jnp.where(lane < 96, right_ok, left_ok))
        return jnp.where(keep > 0.0, placed, 0.0)

    for i, q in ((0, 0), (0, 1), (1, 0), (1, 1)):
        loads[i][q].wait()
    for side, row, rows in ((0, 0, slice(0, RIM)), (1, R - 1, slice(R - RIM, R))):
        edge_out[side, 0:1, :] = u[row : row + 1, :]
        edge_out[side, 1:2, :] = c[row : row + 1, :]
        for p in range(2):
            rim_out[side, p] = conduct_tile(rows, p)
    loads[0][2].wait()
    loads[1][2].wait()
    for load in loads[2]:
        load.wait()

    def owner_ahead(j, start):
        away = half - 1 - j // XL
        return lax.rem(j, XL) * Z + lax.rem(start + away, Z)

    def owner_behind(j, start):
        away = half - 1 - j // XL
        return lax.rem(j, XL) * Z + lax.rem(start + Z - away, Z)

    def packed(ref, p, k):
        here = columns((p * T + k) // 2)
        return pack(ref[0:H, here], ref[H:R, here], lax.rem(k, 2))

    def stage_iterate(j, carry):
        k = owner_ahead(j, z_next)
        for p in range(2):
            u_stage[p, j] = packed(u, p, k)
        return carry

    lax.fori_loop(0, PAIRS, stage_iterate, 0)

    row_of = lax.broadcasted_iota(jnp.int32, (R, LANES), 0)
    lane_r = lane_index((R, LANES))

    def partial(tile, carry):
        here = columns(tile)
        before, after = columns(lax.rem(tile + T - 1, T)), columns(lax.rem(tile + 1, T))
        inner_left, inner_right = flag(tile > 0), flag(tile < T - 1)

        def around(ref):
            middle = ref[:, here]
            left = jnp.where(lane_r == 0, roll(ref[:, before], 1) * inner_left, roll(middle, 1))
            right = jnp.where(
                lane_r == LANES - 1, roll(ref[:, after], -1) * inner_right, roll(middle, -1)
            )
            return middle, (left, right)

        value, value_near = around(u)
        cond, cond_near = around(c)
        total = s[:, here] - value
        for near_value, near_cond in zip(value_near, cond_near):
            total = total + 0.5 * (cond + near_cond) * (near_value - value)
        flow = 0.5 * (cond + pltpu.roll(cond, 1, 0)) * (pltpu.roll(value, 1, 0) - value)
        flow = jnp.where(row_of == 0, 0.0, flow)
        part[:, here] = total + flow - pltpu.roll(flow, R - 1, 0)
        return carry

    lax.fori_loop(0, T, partial, 0)
    beside = sum(jnp.where(exists, 1, 0) for exists, row in there)
    pl.semaphore_wait(barrier, T - 1 + 3 * beside)

    def when_there(side, action):
        pl.when(there[side][0])(action)

    def side_copies(src, dst, send, recv):
        return [
            remote(src.at[side], dst.at[1 - side], send.at[side], recv.at[side], n, there[side][1])
            for side in range(2)
        ]

    edge_copies = side_copies(edge_out, edge_in, edge_send, edge_recv)
    rim_copies = side_copies(rim_out, rim_in, rim_send, rim_recv)
    for copies in (edge_copies, rim_copies):
        for side in range(2):
            when_there(side, copies[side].start)
            finish.append(functools.partial(when_there, side, copies[side].wait_send))

    def u_copy(p, piece):
        some = pl.ds(piece * PIECE, PIECE)
        return remote(
            u_stage.at[p, some], from_prev.at[p, some], u_send, prev_recv.at[p, piece], nxt, sp
        )

    def s_copy(p, piece):
        some = pl.ds(piece * PIECE, PIECE)
        return remote(
            s_stage.at[p, some], from_next.at[p, some], s_send, next_recv.at[p, piece], prv, sp
        )

    for p in range(2):
        for piece in range(PIECES):
            u_copy(p, piece).start()
    for side, row, has in ((0, 0, has_above), (1, R - 1, has_below)):
        when_there(side, edge_copies[1 - side].wait_recv)
        value, cond = u[row : row + 1, :], c[row : row + 1, :]
        value_near = jnp.where(has + jnp.zeros_like(value) > 0.0, edge_in[side, 0:1, :], 0.0)
        cond_near = jnp.where(has + jnp.zeros_like(value) > 0.0, edge_in[side, 1:2, :], 0.0)
        part[row : row + 1, :] = part[row : row + 1, :] + 0.5 * (cond + cond_near) * (
            value_near - value
        )
    for p in range(2):
        def send_partial(piece, carry, p=p):
            for i in range(PIECE):
                j = piece * PIECE + i
                s_stage[p, j] = packed(part, p, owner_behind(j, z_prev))
            s_copy(p, piece).start()
            return carry

        lax.fori_loop(0, PIECES, send_partial, 0)
    finish.append(pltpu.make_async_copy(u_stage, u_stage, u_send).wait)
    finish.append(pltpu.make_async_copy(s_stage, s_stage, s_send).wait)

    def forward_copy(src, p, step, k):
        return remote(src, gathered.at[p, step], fwd_send, fwd_recv.at[p, step], k, sp)

    def forward(src, p, step, k):
        @pl.when(k != n)
        def _():
            forward_copy(src, p, step, k).start()

        @pl.when(k == n)
        def _():
            pltpu.make_async_copy(src, gathered.at[p, step], fwd_recv.at[p, step]).start()

    is_first, is_last = flag(n > 0), flag(n < T - 1)

    def forward_behind(p, j, k, prepare, start):
        if prepare:
            from_next[p, j] = from_next[p, j] + packed(u, p, k) * is_last
        if start:
            forward(from_next.at[p, j], p, nxt, k)

    def forward_ahead(p, j, k, prepare, start):
        if prepare:
            from_prev[p, j] = from_prev[p, j] * is_first + packed(part, p, k)
        if start:
            forward(from_prev.at[p, j], p, n, k)

    def forward_all(p, only=None, prepare=True, start=True, wait=True):
        def one_piece(piece, carry):
            if wait:
                s_copy(p, piece).wait_recv()
                u_copy(p, piece).wait_recv()
            for i in range(PIECE):
                j = piece * PIECE + i
                for owner, send in (
                    (owner_behind, forward_behind), (owner_ahead, forward_ahead)
                ):
                    k = owner(j, z)
                    go = functools.partial(send, p, j, k, prepare, start)
                    if only is None:
                        go()
                    else:
                        pl.when((k == 0) == only)(go)
            return carry

        lax.fori_loop(0, PIECES, one_piece, 0)

    forward_all(0)
    forward_all(1, start=False)
    forward_all(1, only=True, prepare=False, wait=False)
    sent = gathered.at[:, pl.ds(0, T - 2)]
    finish.append(pltpu.make_async_copy(sent, sent, fwd_send).wait)

    for side in range(2):
        when_there(side, rim_copies[1 - side].wait_recv)
    tile_zero = jnp.zeros((RIM, LANES), F32)
    lane_e = lane_index((E, LANES))
    grid_row = sp * R - RIM + lax.broadcasted_iota(jnp.int32, (E, LANES), 0)
    row_ok = jnp.where(grid_row >= 0, 1.0, 0.0) * jnp.where(grid_row < S * R, 1.0, 0.0)
    for p in range(2):
        cond_buf[base : base + RIM, :] = jnp.where(tile_zero + has_above > 0.0, rim_in[0, p], 0.0)
        cond_buf[own : own + R, :] = conduct_tile(slice(0, R), p)
        cond_buf[own + R : own + R + RIM, :] = jnp.where(tile_zero + has_below > 0.0, rim_in[1, p], 0.0)
        block = p * T + n
        right_ok, left_ok = flag(block < 2 * T - 1), flag(block > 0)
        ok = row_ok * jnp.where(lane_e < WIDTH, 1.0, jnp.where(lane_e < 96, right_ok, left_ok))
        middle = cond_buf[base : base + E, :]
        up, down = cond_buf[base - 1 : base + E - 1, :], cond_buf[base + 1 : base + E + 1, :]
        faces = [0.5 * (middle + near) for near in (up, down, roll(middle, 1), roll(middle, -1))]
        g = 1.0 / (1.0 + (faces[0] + faces[1] + faces[2] + faces[3]))
        for i, face in enumerate(faces):
            coeff[p, i] = jnp.where(ok > 0.0, OMEGA * g * face, 0.0)
        coeff[p, 4] = g
        power = g
        count = 1
        while count < T:
            power = power * power
            count *= 2
        coeff[p, 5] = ALPHA / (1.0 - ALPHA * power)
        coeff[p, 6] = jnp.where(ok > 0.0, OMEGA * g, 0.0)

    lane_8 = lane_index((8, LANES))
    segment, in_first = lane_8 // 16, lax.rem(lane_8, 16) < 8
    in_low = lane_8 < WIDTH

    def halo_copies(p):
        right, left = jnp.where(n == T - 1, 0, p), jnp.where(n == 0, 1, p)
        sided = [
            [
                remote(src, dst, halo_send.at[side], recv, step, there[side][1])
                for src, dst, recv, step in (
                    (rows_out.at[p, side], rows_in.at[p, 1 - side], row_recv.at[p, side], n),
                    (right_out.at[right, side], right_in.at[p, 2 + side],
                     corner_recv.at[p, side, 0], nxt),
                    (left_out.at[left, side], left_in.at[p, 2 + side],
                     corner_recv.at[p, side, 1], prv),
                )
            ]
            for side in range(2)
        ]
        level = [
            remote(right_out.at[right], right_in.at[p, pl.ds(0, 2)],
                   col_send, col_recv.at[p, 0], nxt, sp),
            remote(left_out.at[left], left_in.at[p, pl.ds(0, 2)],
                   col_send, col_recv.at[p, 1], prv, sp),
        ]
        return sided, level

    def make_halo(p):
        def one_group(group, carry):
            for j in range(8):
                forward_copy(gathered.at[p, 0], p, group * 8 + j, nxt).wait_recv()
            for j in range(4):
                step = group * 8 + 2 * j
                top, top_next = gathered[p, step, 0:8], gathered[p, step + 1, 0:8]
                rows_out[p, 0, group, j] = jnp.where(in_low, top, roll(top_next, WIDTH))
                bottom = gathered[p, step, H - 8 : H]
                bottom_next = gathered[p, step + 1, H - 8 : H]
                rows_out[p, 1, group, j] = jnp.where(in_low, roll(bottom, WIDTH), bottom_next)
            for i in range(2):
                first = jnp.zeros((8, LANES), F32)
                second = first
                for j in range(8):
                    value = gathered[p, group * 8 + j, 8 * i : 8 * i + 8]
                    first = jnp.where(segment == j, roll(value, 16 * j - 56), first)
                    second = jnp.where(segment == j, roll(value, 16 * j + 8), second)
                right_out[p, i, group] = jnp.where(in_first, first, roll(second, 8))
                left_out[p, i, group] = jnp.where(in_first, roll(first, -8), second)
            return carry

        lax.fori_loop(0, T // 8, one_group, 0)

    def send_halo(p):
        sided, level = halo_copies(p)
        for side in range(2):
            for copy in sided[side]:
                when_there(side, copy.start)
        for copy in level:
            copy.start()

    def wait_halo(p):
        sided, level = halo_copies(p)
        for side in range(2):
            for copy in sided[side]:
                when_there(1 - side, copy.wait_recv)
        for copy in level:
            copy.wait_recv()

    def packed_rows(p, group, j, i):
        if i < 2:
            return gathered[p, group * 8 + j, 8 * i : 8 * i + 8]
        down, up = rows_in[p, 1, group, j // 2], rows_in[p, 0, group, j // 2]
        if j % 2:
            return jnp.where(in_low, roll(down, WIDTH), up)
        return jnp.where(in_low, down, roll(up, WIDTH))

    def packed_columns(p, group, i):
        if i < 2:
            return right_in[p, i, group], left_in[p, i, group]
        return (
            jnp.where(in_first, right_in[p, 2, group], right_in[p, 3, group]),
            jnp.where(in_first, left_in[p, 3, group], left_in[p, 2, group]),
        )

    GROUPS = ((0, 2), (1, 3), (4, -1))

    def unpack(p):
        def unpack_group(group, carry):
            for i, (low, high) in enumerate(GROUPS):
                from_left, from_right = packed_columns(p, group, i)
                for j in range(8):
                    step = group * 8 + j
                    value = packed_rows(p, group, j, i)
                    for place, own_part, left_at, right_at in (
                        (low, value, 0, 8),
                        (high, roll(value, WIDTH), 8, 0),
                    ):
                        left = roll(from_left, 120 - 16 * j - left_at)
                        right = roll(from_right, 64 - 16 * j - right_at)
                        x_buf[step, own + 8 * place : own + 8 * place + 8, :] = jnp.where(
                            in_low, own_part, jnp.where(lane_8 < 96, right, left)
                        )
            return carry

        lax.fori_loop(0, T // 8, unpack_group, 0)

    def over_time(body, carry):
        for step in range(T):
            carry = body(step, carry)
        return carry

    def wrap(p, first, rows, dst, last):
        here = pl.ds(base + first, rows)
        gain = coeff[p, 4, first : first + rows, :]

        def body(t, carry):
            carry = gain * carry
            dst[t, here, :] = dst[t, here, :] + carry
            return carry

        over_time(body, last * coeff[p, 5, first : first + rows, :])

    def first_sweep(p, first, rows, src, dst):
        here, q_here = pl.ds(base + first, rows), pl.ds(first, rows)
        gain = coeff[p, 4, first : first + rows, :]
        weight = coeff[p, 6, first : first + rows, :]
        ok = weight > 0.0

        def body(t, carry):
            scaled = jnp.where(ok, weight * src[t, here, :], 0.0)
            q_buf[t, q_here, :] = scaled
            value = scaled + gain * carry
            dst[t, here, :] = value
            return value

        last = over_time(body, jnp.zeros((rows, LANES), F32))
        wrap(p, first, rows, dst, last)

    def sweep(p, first, rows, src, dst):
        here, q_here = pl.ds(base + first, rows), pl.ds(first, rows)
        here_up, here_down = pl.ds(base + first - 1, rows), pl.ds(base + first + 1, rows)
        k = [coeff[p, i, first : first + rows, :] for i in range(5)]

        def body(t, carry):
            mine = src[t, here, :]
            near = k[0] * src[t, here_up, :] + k[1] * src[t, here_down, :]
            near = near + (k[2] * roll(mine, 1) + k[3] * roll(mine, -1))
            value = (q_buf[t, q_here, :] + near) + k[4] * carry
            dst[t, here, :] = (1.0 - OMEGA) * mine + value
            return value

        last = over_time(body, jnp.zeros((rows, LANES), F32))
        wrap(p, first, rows, dst, last)

    def blocks_of(first, stop, rows):
        return [(at, min(rows, stop - at)) for at in range(first, stop, rows)]

    BLOCK = 24

    def solve(p):
        for first, rows in blocks_of(0, E, BLOCK):
            first_sweep(p, first, rows, x_buf, w_buf)

        def two_sweeps(i, carry):
            for first, rows in blocks_of(0, E, BLOCK):
                sweep(p, first, rows, w_buf, x_buf)
            for first, rows in blocks_of(0, E, BLOCK):
                sweep(p, first, rows, x_buf, w_buf)
            return carry

        lax.fori_loop(0, (SWEEPS - 2) // 2, two_sweeps, 0)
        for first, rows in blocks_of(RIM, RIM + R, 16):
            sweep(p, first, rows, w_buf, x_buf)

    def back_copy(p, step, k):
        return remote(back_out.at[p, step], back_in.at[p, k], back_send, back_recv.at[p, k], step, sp)

    def pack_back(p):
        lane = lane_index((H, LANES))

        def pack_steps(group, carry):
            for j in range(8):
                step = group * 8 + j
                low, high = x_buf[step, own : own + H, :], x_buf[step, own + H : own + R, :]
                back_out[p, step] = jnp.where(lane < WIDTH, low, roll(high, WIDTH))
            return carry

        lax.fori_loop(0, T // 8, pack_steps, 0)

    def give_back(p, start, stop):
        def send(j, carry):
            m = j // XL
            away = half - (m + 1) // 2
            toward = jnp.where(lax.rem(m, 2) == 1, away, Z - away)
            step = lax.rem(j, XL) * Z + lax.rem(z + toward, Z)

            @pl.when(step != n)
            def _():
                back_copy(p, step, n).start()

            @pl.when(step == n)
            def _():
                pltpu.make_async_copy(
                    back_out.at[p, step], back_in.at[p, n], back_recv.at[p, n]
                ).start()

            return carry

        lax.fori_loop(start, stop, send, 0)

    def store_copy(tile):
        return pltpu.make_async_copy(out.at[:, columns(tile)], out_hbm.at[:, columns(tile)], store_sem)

    def update(p):
        lane = lane_index((H, LANES))

        def step(j, carry):
            m = j // XL
            away = half // 2 - (m + 1) // 2
            toward = jnp.where(lax.rem(m, 2) == 1, away, half - away)
            pair = lax.rem(j, XL) * half + lax.rem(z // 2 + toward, half)
            for k in (2 * pair, 2 * pair + 1):
                back_copy(p, nxt, k).wait_recv()
            even, odd = back_in[p, 2 * pair], back_in[p, 2 * pair + 1]
            tile = p * PAIRS + pair
            here = columns(tile)
            out[0:H, here] = u[0:H, here] + jnp.where(lane < WIDTH, even, roll(odd, WIDTH))
            out[H:R, here] = u[H:R, here] + jnp.where(lane < WIDTH, roll(even, WIDTH), odd)
            store_copy(tile).start()
            return carry

        lax.fori_loop(0, PAIRS, step, 0)

    EARLY = 4

    pl.when(n == 0)(lambda: make_halo(1))
    make_halo(0)
    send_halo(0)
    forward_all(1, only=False, prepare=False, wait=False)
    wait_halo(0)
    unpack(0)
    solve(0)
    pack_back(0)

    give_back(0, 0, EARLY)
    pl.when(n != 0)(lambda: make_halo(1))
    send_halo(1)
    give_back(0, EARLY, T)
    wait_halo(1)
    unpack(1)
    solve(1)
    pack_back(1)
    give_back(1, 0, T)
    update(0)
    update(1)
    finish.append(pltpu.make_async_copy(right_in, right_in, col_send).wait)
    for side in range(2):
        for sent in (rows_out.at[0], right_out):
            wait = pltpu.make_async_copy(sent, sent, halo_send.at[side]).wait
            finish.append(functools.partial(when_there, side, wait))
    sent = back_out.at[:, pl.ds(0, T - 1)]
    finish.append(pltpu.make_async_copy(sent, sent, back_send).wait)
    finish.append(pltpu.make_async_copy(out, out, store_sem).wait)
    for wait in finish:
        wait()


def per_device(iterate, source, conduct):
    T, S = lax.axis_size("tm"), lax.axis_size("space")
    R, NC = conduct.shape
    Z = T // 2
    E = R + 2 * RIM
    dma = pltpu.SemaphoreType.DMA
    vmem = lambda *shape: pltpu.VMEM(shape, F32)
    block = (R // 2, LANES)
    tile = (8, LANES)
    in_hbm = pl.BlockSpec(memory_space=pltpu.HBM)
    updated = pl.pallas_call(
        functools.partial(kernel, T, S, Z, R),
        out_shape=jax.ShapeDtypeStruct((R, NC), F32),
        in_specs=[in_hbm] * 3,
        out_specs=in_hbm,
        scratch_shapes=[
            vmem(R, NC), vmem(R, NC), vmem(R, NC), vmem(R, NC), vmem(R, NC),
            vmem(2, 2, NC), vmem(2, 2, NC), vmem(2, 2, RIM, LANES), vmem(2, 2, RIM, LANES),
            vmem(2, T // 2, *block), vmem(2, T // 2, *block),
            vmem(2, T // 2, *block), vmem(2, T // 2, *block),
            vmem(2, T, *block), vmem(2, 2, T // 8, 4, RIM, LANES), vmem(2, 2, T // 8, 4, RIM, LANES),
            vmem(2, 2, T // 8, *tile), vmem(2, 2, T // 8, *tile),
            vmem(2, 4, T // 8, *tile), vmem(2, 4, T // 8, *tile),
            vmem(T, E + 16, LANES), vmem(T, E + 16, LANES), vmem(T, E, LANES),
            vmem(E + 16, LANES), vmem(2, 7, E, LANES),
            vmem(2, T, *block), vmem(2, T, *block),
            dma((3, 3)), dma, dma((2,)), dma((2,)), dma((2,)), dma((2,)),
            dma, dma, dma((2, 4)), dma((2, 4)),
            dma, dma((2, T)), dma((2,)), dma((2, 2)), dma, dma((2, 2)), dma((2, 2, 2)),
            dma, dma((2, T)),
        ],
        compiler_params=pltpu.CompilerParams(
            collective_id=0, has_side_effects=True, vmem_limit_bytes=60 * 1024 * 1024
        ),
    )(iterate[0], source[0], conduct)
    return updated[None]


def solution(mesh):
    return jax.shard_map(
        per_device,
        mesh=mesh,
        in_specs=(P("tm", "space", None), P("tm", "space", None), P("space", None)),
        out_specs=P("tm", "space", None),
        check_vma=False,
    )
```

```python
import functools

import jax
import jax.numpy as jnp
from jax import lax
from jax.experimental import pallas as pl
from jax.experimental.pallas import tpu as pltpu
from jax.sharding import PartitionSpec as P

ALPHA = 0.05
OMEGA = 0.8
SWEEPS = 8
LANES = 128
WIDTH = 64
RIM = 8
MESH = pl.DeviceIdType.MESH
F32 = jnp.float32


def lane_index(shape):
    return lax.broadcasted_iota(jnp.int32, shape, len(shape) - 1)


def roll(value, shift):
    shift = shift % LANES
    return pltpu.roll(value, shift, value.ndim - 1) if shift else value


def flag(condition):
    return jnp.where(condition, 1.0, 0.0).astype(F32)


def kernel(
    T, S, Z, R,
    u_hbm, s_hbm, c_hbm, out_hbm,
    u, s, c, out, part,
    edge_out, edge_in, rim_out, rim_in,
    u_stage, s_stage, from_prev, from_next,
    gathered, rows_out, rows_in, right_out, left_out, right_in, left_in,
    x_buf, w_buf, q_buf, cond_buf, coeff,
    back_out, back_in,
    load_sem, store_sem, edge_send, edge_recv, rim_send, rim_recv,
    u_send, s_send, prev_recv, next_recv,
    fwd_send, fwd_recv, halo_send, row_recv, col_send, col_recv, corner_recv,
    back_send, back_recv,
):
    n, sp = lax.axis_index("tm"), lax.axis_index("space")
    XL = T // Z
    half = Z // 2
    z = lax.rem(n, Z)
    z_next, z_prev = lax.rem(z + 1, Z), lax.rem(z + Z - 1, Z)
    nxt, prv = lax.rem(n + 1, T), lax.rem(n + T - 1, T)
    below, above = lax.rem(sp + 1, S), lax.rem(sp + S - 1, S)
    has_above, has_below = flag(sp > 0), flag(sp < S - 1)
    H = R // 2
    E = R + 2 * RIM
    base = RIM
    own = base + RIM
    PAIRS = T // 2
    PIECES = 4
    PIECE = PAIRS // PIECES

    finish = []
    loads = []
    pieces = [(0, RIM), (R - RIM, RIM), (RIM, R - 2 * RIM)]
    for i, (a, b) in enumerate(((u_hbm, u), (c_hbm, c), (s_hbm, s))):
        loads.append([
            pltpu.make_async_copy(a.at[pl.ds(at, rows)], b.at[pl.ds(at, rows)], load_sem.at[i, q])
            for q, (at, rows) in enumerate(pieces)
        ])
    for group in ((0, 0), (0, 1), (1, 0), (1, 1), (0, 2), (1, 2), (2, 0), (2, 1), (2, 2)):
        loads[group[0]][group[1]].start()

    barrier = pltpu.get_barrier_semaphore()

    def greet(i, carry):
        pl.semaphore_signal(
            barrier, inc=1, device_id=(lax.rem(n + i, T), sp), device_id_type=MESH
        )
        return carry

    lax.fori_loop(1, T, greet, 0)
    there = ((sp > 0, above), (sp < S - 1, below))
    for exists, row in there:
        @pl.when(exists)
        def _(row=row):
            for step in (prv, n, nxt):
                pl.semaphore_signal(barrier, inc=1, device_id=(step, row), device_id_type=MESH)

    def columns(tile):
        return pl.ds(pl.multiple_of(tile * LANES, LANES), LANES)

    def remote(src, dst, send, recv, step, row):
        return pltpu.make_async_remote_copy(
            src_ref=src, dst_ref=dst, send_sem=send, recv_sem=recv,
            device_id=(step, row), device_id_type=MESH,
        )

    def pack(low, high, odd):
        lane = lane_index(low.shape)
        is_odd = jnp.zeros(low.shape, jnp.int32) + odd
        kept = jnp.where(is_odd == 1, high, low)
        moved = roll(jnp.where(is_odd == 1, low, high), WIDTH)
        return jnp.where(lane // WIDTH == is_odd, kept, moved)

    def conduct_tile(rows, half_index):
        block = half_index * T + n
        tile, odd = block // 2, lax.rem(block, 2)
        first = c[rows, columns(lax.rem(tile + odd, T))]
        second = c[rows, columns(lax.rem(tile + odd + T - 1, T))]
        lane = lane_index(first.shape)
        is_odd = jnp.zeros(first.shape, jnp.int32) + odd
        joined = jnp.where(lane < 96 - WIDTH * is_odd, first, second)
        placed = jnp.where(is_odd == 1, roll(joined, WIDTH), joined)
        right_ok, left_ok = flag(block < 2 * T - 1), flag(block > 0)
        keep = jnp.where(lane < WIDTH, 1.0, jnp.where(lane < 96, right_ok, left_ok))
        return jnp.where(keep > 0.0, placed, 0.0)

    for i, q in ((0, 0), (0, 1), (1, 0), (1, 1)):
        loads[i][q].wait()
    for side, row, rows in ((0, 0, slice(0, RIM)), (1, R - 1, slice(R - RIM, R))):
        edge_out[side, 0:1, :] = u[row : row + 1, :]
        edge_out[side, 1:2, :] = c[row : row + 1, :]
        for p in range(2):
            rim_out[side, p] = conduct_tile(rows, p)
    loads[0][2].wait()
    loads[1][2].wait()
    for load in loads[2]:
        load.wait()

    def owner_ahead(j, start):
        away = half - 1 - j // XL
        return lax.rem(j, XL) * Z + lax.rem(start + away, Z)

    def owner_behind(j, start):
        away = half - 1 - j // XL
        return lax.rem(j, XL) * Z + lax.rem(start + Z - away, Z)

    def packed(ref, p, k):
        here = columns((p * T + k) // 2)
        return pack(ref[0:H, here], ref[H:R, here], lax.rem(k, 2))

    def stage_iterate(j, carry):
        k = owner_ahead(j, z_next)
        for p in range(2):
            u_stage[p, j] = packed(u, p, k)
        return carry

    lax.fori_loop(0, PAIRS, stage_iterate, 0)

    row_of = lax.broadcasted_iota(jnp.int32, (R, LANES), 0)
    lane_r = lane_index((R, LANES))

    def partial(tile, carry):
        here = columns(tile)
        before, after = columns(lax.rem(tile + T - 1, T)), columns(lax.rem(tile + 1, T))
        inner_left, inner_right = flag(tile > 0), flag(tile < T - 1)

        def around(ref):
            middle = ref[:, here]
            left = jnp.where(lane_r == 0, roll(ref[:, before], 1) * inner_left, roll(middle, 1))
            right = jnp.where(
                lane_r == LANES - 1, roll(ref[:, after], -1) * inner_right, roll(middle, -1)
            )
            return middle, (left, right)

        value, value_near = around(u)
        cond, cond_near = around(c)
        total = s[:, here] - value
        for near_value, near_cond in zip(value_near, cond_near):
            total = total + 0.5 * (cond + near_cond) * (near_value - value)
        flow = 0.5 * (cond + pltpu.roll(cond, 1, 0)) * (pltpu.roll(value, 1, 0) - value)
        flow = jnp.where(row_of == 0, 0.0, flow)
        part[:, here] = total + flow - pltpu.roll(flow, R - 1, 0)
        return carry

    lax.fori_loop(0, T, partial, 0)
    beside = sum(jnp.where(exists, 1, 0) for exists, row in there)
    pl.semaphore_wait(barrier, T - 1 + 3 * beside)

    def when_there(side, action):
        pl.when(there[side][0])(action)

    def side_copies(src, dst, send, recv):
        return [
            remote(src.at[side], dst.at[1 - side], send.at[side], recv.at[side], n, there[side][1])
            for side in range(2)
        ]

    edge_copies = side_copies(edge_out, edge_in, edge_send, edge_recv)
    rim_copies = side_copies(rim_out, rim_in, rim_send, rim_recv)
    for copies in (edge_copies, rim_copies):
        for side in range(2):
            when_there(side, copies[side].start)
            finish.append(functools.partial(when_there, side, copies[side].wait_send))

    def u_copy(p, piece):
        some = pl.ds(piece * PIECE, PIECE)
        return remote(
            u_stage.at[p, some], from_prev.at[p, some], u_send, prev_recv.at[p, piece], nxt, sp
        )

    def s_copy(p, piece):
        some = pl.ds(piece * PIECE, PIECE)
        return remote(
            s_stage.at[p, some], from_next.at[p, some], s_send, next_recv.at[p, piece], prv, sp
        )

    for p in range(2):
        for piece in range(PIECES):
            u_copy(p, piece).start()
    for side, row, has in ((0, 0, has_above), (1, R - 1, has_below)):
        when_there(side, edge_copies[1 - side].wait_recv)
        value, cond = u[row : row + 1, :], c[row : row + 1, :]
        value_near = jnp.where(has + jnp.zeros_like(value) > 0.0, edge_in[side, 0:1, :], 0.0)
        cond_near = jnp.where(has + jnp.zeros_like(value) > 0.0, edge_in[side, 1:2, :], 0.0)
        part[row : row + 1, :] = part[row : row + 1, :] + 0.5 * (cond + cond_near) * (
            value_near - value
        )
    for p in range(2):
        def send_partial(piece, carry, p=p):
            for i in range(PIECE):
                j = piece * PIECE + i
                s_stage[p, j] = packed(part, p, owner_behind(j, z_prev))
            s_copy(p, piece).start()
            return carry

        lax.fori_loop(0, PIECES, send_partial, 0)
    finish.append(pltpu.make_async_copy(u_stage, u_stage, u_send).wait)
    finish.append(pltpu.make_async_copy(s_stage, s_stage, s_send).wait)

    def forward_copy(src, p, step, k):
        return remote(src, gathered.at[p, step], fwd_send, fwd_recv.at[p, step], k, sp)

    def forward(src, p, step, k):
        @pl.when(k != n)
        def _():
            forward_copy(src, p, step, k).start()

        @pl.when(k == n)
        def _():
            pltpu.make_async_copy(src, gathered.at[p, step], fwd_recv.at[p, step]).start()

    is_first, is_last = flag(n > 0), flag(n < T - 1)

    def forward_behind(p, j, k, prepare, start):
        if prepare:
            from_next[p, j] = from_next[p, j] + packed(u, p, k) * is_last
        if start:
            forward(from_next.at[p, j], p, nxt, k)

    def forward_ahead(p, j, k, prepare, start):
        if prepare:
            from_prev[p, j] = from_prev[p, j] * is_first + packed(part, p, k)
        if start:
            forward(from_prev.at[p, j], p, n, k)

    def forward_all(p, only=None, prepare=True, start=True, wait=True):
        def one_piece(piece, carry):
            if wait:
                s_copy(p, piece).wait_recv()
                u_copy(p, piece).wait_recv()
            for i in range(PIECE):
                j = piece * PIECE + i
                for owner, send in (
                    (owner_behind, forward_behind), (owner_ahead, forward_ahead)
                ):
                    k = owner(j, z)
                    go = functools.partial(send, p, j, k, prepare, start)
                    if only is None:
                        go()
                    else:
                        pl.when((k == 0) == only)(go)
            return carry

        lax.fori_loop(0, PIECES, one_piece, 0)

    forward_all(0)
    forward_all(1, start=False)
    forward_all(1, only=True, prepare=False, wait=False)
    sent = gathered.at[:, pl.ds(0, T - 2)]
    finish.append(pltpu.make_async_copy(sent, sent, fwd_send).wait)

    for side in range(2):
        when_there(side, rim_copies[1 - side].wait_recv)
    tile_zero = jnp.zeros((RIM, LANES), F32)
    lane_e = lane_index((E, LANES))
    grid_row = sp * R - RIM + lax.broadcasted_iota(jnp.int32, (E, LANES), 0)
    row_ok = jnp.where(grid_row >= 0, 1.0, 0.0) * jnp.where(grid_row < S * R, 1.0, 0.0)
    for p in range(2):
        cond_buf[base : base + RIM, :] = jnp.where(tile_zero + has_above > 0.0, rim_in[0, p], 0.0)
        cond_buf[own : own + R, :] = conduct_tile(slice(0, R), p)
        cond_buf[own + R : own + R + RIM, :] = jnp.where(tile_zero + has_below > 0.0, rim_in[1, p], 0.0)
        block = p * T + n
        right_ok, left_ok = flag(block < 2 * T - 1), flag(block > 0)
        ok = row_ok * jnp.where(lane_e < WIDTH, 1.0, jnp.where(lane_e < 96, right_ok, left_ok))
        middle = cond_buf[base : base + E, :]
        up, down = cond_buf[base - 1 : base + E - 1, :], cond_buf[base + 1 : base + E + 1, :]
        faces = [0.5 * (middle + near) for near in (up, down, roll(middle, 1), roll(middle, -1))]
        g = 1.0 / (1.0 + (faces[0] + faces[1] + faces[2] + faces[3]))
        for i, face in enumerate(faces):
            coeff[p, i] = jnp.where(ok > 0.0, OMEGA * g * face, 0.0)
        coeff[p, 4] = g
        power = g
        count = 1
        while count < T:
            power = power * power
            count *= 2
        coeff[p, 5] = ALPHA / (1.0 - ALPHA * power)
        coeff[p, 6] = jnp.where(ok > 0.0, OMEGA * g, 0.0)

    lane_8 = lane_index((8, LANES))
    segment, in_first = lane_8 // 16, lax.rem(lane_8, 16) < 8
    in_low = lane_8 < WIDTH

    def halo_copies(p):
        right, left = jnp.where(n == T - 1, 0, p), jnp.where(n == 0, 1, p)
        sided = [
            [
                remote(src, dst, halo_send.at[side], recv, step, there[side][1])
                for src, dst, recv, step in (
                    (rows_out.at[p, side], rows_in.at[p, 1 - side], row_recv.at[p, side], n),
                    (right_out.at[right, side], right_in.at[p, 2 + side],
                     corner_recv.at[p, side, 0], nxt),
                    (left_out.at[left, side], left_in.at[p, 2 + side],
                     corner_recv.at[p, side, 1], prv),
                )
            ]
            for side in range(2)
        ]
        level = [
            remote(right_out.at[right], right_in.at[p, pl.ds(0, 2)],
                   col_send, col_recv.at[p, 0], nxt, sp),
            remote(left_out.at[left], left_in.at[p, pl.ds(0, 2)],
                   col_send, col_recv.at[p, 1], prv, sp),
        ]
        return sided, level

    def make_halo(p):
        def one_group(group, carry):
            for j in range(8):
                forward_copy(gathered.at[p, 0], p, group * 8 + j, nxt).wait_recv()
            for j in range(4):
                step = group * 8 + 2 * j
                top, top_next = gathered[p, step, 0:8], gathered[p, step + 1, 0:8]
                rows_out[p, 0, group, j] = jnp.where(in_low, top, roll(top_next, WIDTH))
                bottom = gathered[p, step, H - 8 : H]
                bottom_next = gathered[p, step + 1, H - 8 : H]
                rows_out[p, 1, group, j] = jnp.where(in_low, roll(bottom, WIDTH), bottom_next)
            for i in range(2):
                first = jnp.zeros((8, LANES), F32)
                second = first
                for j in range(8):
                    value = gathered[p, group * 8 + j, 8 * i : 8 * i + 8]
                    first = jnp.where(segment == j, roll(value, 16 * j - 56), first)
                    second = jnp.where(segment == j, roll(value, 16 * j + 8), second)
                right_out[p, i, group] = jnp.where(in_first, first, roll(second, 8))
                left_out[p, i, group] = jnp.where(in_first, roll(first, -8), second)
            return carry

        lax.fori_loop(0, T // 8, one_group, 0)

    def send_halo(p):
        sided, level = halo_copies(p)
        for side in range(2):
            for copy in sided[side]:
                when_there(side, copy.start)
        for copy in level:
            copy.start()

    def wait_halo(p):
        sided, level = halo_copies(p)
        for side in range(2):
            for copy in sided[side]:
                when_there(1 - side, copy.wait_recv)
        for copy in level:
            copy.wait_recv()

    def packed_rows(p, group, j, i):
        if i < 2:
            return gathered[p, group * 8 + j, 8 * i : 8 * i + 8]
        down, up = rows_in[p, 1, group, j // 2], rows_in[p, 0, group, j // 2]
        if j % 2:
            return jnp.where(in_low, roll(down, WIDTH), up)
        return jnp.where(in_low, down, roll(up, WIDTH))

    def packed_columns(p, group, i):
        if i < 2:
            return right_in[p, i, group], left_in[p, i, group]
        return (
            jnp.where(in_first, right_in[p, 2, group], right_in[p, 3, group]),
            jnp.where(in_first, left_in[p, 3, group], left_in[p, 2, group]),
        )

    GROUPS = ((0, 2), (1, 3), (4, -1))

    def over_time(body, carry):
        for step in range(T):
            carry = body(step, carry)
        return carry

    def wrap(p, first, rows, dst, last):
        here = pl.ds(base + first, rows)
        gain = coeff[p, 4, first : first + rows, :]

        def body(t, carry):
            carry = gain * carry
            dst[t, here, :] = dst[t, here, :] + carry
            return carry

        over_time(body, last * coeff[p, 5, first : first + rows, :])

    def first_sweep(p):
        places = [place for pair in GROUPS for place in pair]
        firsts = [RIM + 8 * place for place in places]
        gains = [coeff[p, 4, first : first + 8, :] for first in firsts]
        weights = [coeff[p, 6, first : first + 8, :] for first in firsts]

        def one_group(group, carry):
            carry = list(carry)
            for i in range(3):
                from_left, from_right = packed_columns(p, group, i)
                for j in range(8):
                    step = group * 8 + j
                    value = packed_rows(p, group, j, i)
                    for at, own_part, left_at, right_at in (
                        (2 * i, value, 0, 8),
                        (2 * i + 1, roll(value, WIDTH), 8, 0),
                    ):
                        left = roll(from_left, 120 - 16 * j - left_at)
                        right = roll(from_right, 64 - 16 * j - right_at)
                        whole = jnp.where(in_low, own_part, jnp.where(lane_8 < 96, right, left))
                        scaled = jnp.where(weights[at] > 0.0, weights[at] * whole, 0.0)
                        first = firsts[at]
                        q_buf[step, first : first + 8, :] = scaled
                        carry[at] = scaled + gains[at] * carry[at]
                        w_buf[step, base + first : base + first + 8, :] = carry[at]
            return tuple(carry)

        zero = jnp.zeros((8, LANES), F32)
        last = lax.fori_loop(0, T // 8, one_group, (zero,) * len(places))
        in_order = sorted(zip(firsts, last), key=lambda pair: pair[0])
        wrap(p, 0, E, w_buf, jnp.concatenate([value for _, value in in_order], axis=0))

    def sweep(p, first, rows, src, dst):
        here, q_here = pl.ds(base + first, rows), pl.ds(first, rows)
        here_up, here_down = pl.ds(base + first - 1, rows), pl.ds(base + first + 1, rows)
        k = [coeff[p, i, first : first + rows, :] for i in range(5)]

        def body(t, carry):
            mine = src[t, here, :]
            near = k[0] * src[t, here_up, :] + k[1] * src[t, here_down, :]
            near = near + (k[2] * roll(mine, 1) + k[3] * roll(mine, -1))
            value = (q_buf[t, q_here, :] + near) + k[4] * carry
            dst[t, here, :] = (1.0 - OMEGA) * mine + value
            return value

        last = over_time(body, jnp.zeros((rows, LANES), F32))
        wrap(p, first, rows, dst, last)

    def blocks_of(first, stop, rows):
        return [(at, min(rows, stop - at)) for at in range(first, stop, rows)]

    BLOCK = 24

    def solve(p):
        first_sweep(p)

        def two_sweeps(i, carry):
            for first, rows in blocks_of(0, E, BLOCK):
                sweep(p, first, rows, w_buf, x_buf)
            for first, rows in blocks_of(0, E, BLOCK):
                sweep(p, first, rows, x_buf, w_buf)
            return carry

        lax.fori_loop(0, (SWEEPS - 2) // 2, two_sweeps, 0)
        for first, rows in blocks_of(RIM, RIM + R, 16):
            sweep(p, first, rows, w_buf, x_buf)

    def back_copy(p, step, k):
        return remote(back_out.at[p, step], back_in.at[p, k], back_send, back_recv.at[p, k], step, sp)

    def pack_back(p):
        lane = lane_index((H, LANES))

        def pack_steps(group, carry):
            for j in range(8):
                step = group * 8 + j
                low, high = x_buf[step, own : own + H, :], x_buf[step, own + H : own + R, :]
                back_out[p, step] = jnp.where(lane < WIDTH, low, roll(high, WIDTH))
            return carry

        lax.fori_loop(0, T // 8, pack_steps, 0)

    def give_back(p, start, stop):
        def send(j, carry):
            m = j // XL
            away = half - (m + 1) // 2
            toward = jnp.where(lax.rem(m, 2) == 1, away, Z - away)
            step = lax.rem(j, XL) * Z + lax.rem(z + toward, Z)

            @pl.when(step != n)
            def _():
                back_copy(p, step, n).start()

            @pl.when(step == n)
            def _():
                pltpu.make_async_copy(
                    back_out.at[p, step], back_in.at[p, n], back_recv.at[p, n]
                ).start()

            return carry

        lax.fori_loop(start, stop, send, 0)

    def store_copy(tile):
        return pltpu.make_async_copy(out.at[:, columns(tile)], out_hbm.at[:, columns(tile)], store_sem)

    def update(p):
        lane = lane_index((H, LANES))

        def step(j, carry):
            m = j // XL
            away = half // 2 - (m + 1) // 2
            toward = jnp.where(lax.rem(m, 2) == 1, away, half - away)
            pair = lax.rem(j, XL) * half + lax.rem(z // 2 + toward, half)
            for k in (2 * pair, 2 * pair + 1):
                back_copy(p, nxt, k).wait_recv()
            even, odd = back_in[p, 2 * pair], back_in[p, 2 * pair + 1]
            tile = p * PAIRS + pair
            here = columns(tile)
            out[0:H, here] = u[0:H, here] + jnp.where(lane < WIDTH, even, roll(odd, WIDTH))
            out[H:R, here] = u[H:R, here] + jnp.where(lane < WIDTH, roll(even, WIDTH), odd)
            store_copy(tile).start()
            return carry

        lax.fori_loop(0, PAIRS, step, 0)

    EARLY = 4

    pl.when(n == 0)(lambda: make_halo(1))
    make_halo(0)
    send_halo(0)
    forward_all(1, only=False, prepare=False, wait=False)
    wait_halo(0)
    solve(0)
    pack_back(0)

    give_back(0, 0, EARLY)
    pl.when(n != 0)(lambda: make_halo(1))
    send_halo(1)
    give_back(0, EARLY, T)
    wait_halo(1)
    solve(1)
    pack_back(1)
    give_back(1, 0, T)
    update(0)
    update(1)
    finish.append(pltpu.make_async_copy(right_in, right_in, col_send).wait)
    for side in range(2):
        for sent in (rows_out.at[0], right_out):
            wait = pltpu.make_async_copy(sent, sent, halo_send.at[side]).wait
            finish.append(functools.partial(when_there, side, wait))
    sent = back_out.at[:, pl.ds(0, T - 1)]
    finish.append(pltpu.make_async_copy(sent, sent, back_send).wait)
    finish.append(pltpu.make_async_copy(out, out, store_sem).wait)
    for wait in finish:
        wait()


def per_device(iterate, source, conduct):
    T, S = lax.axis_size("tm"), lax.axis_size("space")
    R, NC = conduct.shape
    Z = T // 2
    E = R + 2 * RIM
    dma = pltpu.SemaphoreType.DMA
    vmem = lambda *shape: pltpu.VMEM(shape, F32)
    block = (R // 2, LANES)
    tile = (8, LANES)
    in_hbm = pl.BlockSpec(memory_space=pltpu.HBM)
    updated = pl.pallas_call(
        functools.partial(kernel, T, S, Z, R),
        out_shape=jax.ShapeDtypeStruct((R, NC), F32),
        in_specs=[in_hbm] * 3,
        out_specs=in_hbm,
        scratch_shapes=[
            vmem(R, NC), vmem(R, NC), vmem(R, NC), vmem(R, NC), vmem(R, NC),
            vmem(2, 2, NC), vmem(2, 2, NC), vmem(2, 2, RIM, LANES), vmem(2, 2, RIM, LANES),
            vmem(2, T // 2, *block), vmem(2, T // 2, *block),
            vmem(2, T // 2, *block), vmem(2, T // 2, *block),
            vmem(2, T, *block), vmem(2, 2, T // 8, 4, RIM, LANES), vmem(2, 2, T // 8, 4, RIM, LANES),
            vmem(2, 2, T // 8, *tile), vmem(2, 2, T // 8, *tile),
            vmem(2, 4, T // 8, *tile), vmem(2, 4, T // 8, *tile),
            vmem(T, E + 16, LANES), vmem(T, E + 16, LANES), vmem(T, E, LANES),
            vmem(E + 16, LANES), vmem(2, 7, E, LANES),
            vmem(2, T, *block), vmem(2, T, *block),
            dma((3, 3)), dma, dma((2,)), dma((2,)), dma((2,)), dma((2,)),
            dma, dma, dma((2, 4)), dma((2, 4)),
            dma, dma((2, T)), dma((2,)), dma((2, 2)), dma, dma((2, 2)), dma((2, 2, 2)),
            dma, dma((2, T)),
        ],
        compiler_params=pltpu.CompilerParams(
            collective_id=0, has_side_effects=True, vmem_limit_bytes=60 * 1024 * 1024
        ),
    )(iterate[0], source[0], conduct)
    return updated[None]


def solution(mesh):
    return jax.shard_map(
        per_device,
        mesh=mesh,
        in_specs=(P("tm", "space", None), P("tm", "space", None), P("space", None)),
        out_specs=P("tm", "space", None),
        check_vma=False,
    )
```
